512 devices in a mesh: sub: 16 (over z, core), region: 32 (over y, x).
Axes of the slice: x: 4, y: 8, z: 8, core: 2. Of those that a mesh axis runs over, the one named last changes fastest.
Arguments:
- residual: bfloat16 [16, 32, 512, 1024], P('sub', 'region'), may hold values from -6 to 6
- send_rows: int32 [16, 32, 4, 64], P('sub', 'region'), may hold values from 0 to 511
- local_inverse: bfloat16 [16, 32, 512, 768], P('sub', 'region'), may hold values from -0.21875 to 0.21875
- coarse_basis: bfloat16 [16, 32, 512, 128], P('sub', 'region'), may hold values from -0.25 to 0.25
- regional_inverse: bfloat16 [16, 32, 128, 2048], P('sub', 'region'), may hold values from -0.125 to 0.125
- root_map: bfloat16 [16, 32, 128, 64], P('sub', 'region'), may hold values from -0.75 to 0.75
- root_inverse: bfloat16 [32, 64, 2048], P('region'), may hold values from -0.0234375 to 0.0234375
Outputs:
- correction: bfloat16 [16, 32, 512, 1024], P('sub', 'region')
The draws below stay inside these ranges and needn't reach their ends.
All inputs are finite; a program needn't handle non-finite values.
Results may differ from the reference program's by a relative error of at most 0.0055.
Values may be sent and summed in bfloat16 or wider, within the bound.
A program may use at most 64 MiB of HBM per device.

```python
import jax
import jax.numpy as jnp
from jax import lax

SUBN = 768
OV = 64
KC = 128
KR = 64
C = 1024
NOWN = 512
RC = 2048
ROOT = 2048
N_SUB = 16
N_REGION = 32


def place_ends(drawn, rng, least, high):
    index_at = [jax.random.randint(jax.random.fold_in(rng, axis), (), 0, length) for axis, length in enumerate(drawn.shape)]
    widest = drawn.shape.index(max(drawn.shape))
    neighbour = index_at[:widest] + [(index_at[widest] + 1) % drawn.shape[widest]] + index_at[widest + 1:]
    return drawn.at[tuple(index_at)].set(least).at[tuple(neighbour)].set(high)


def levels(key, shape, split, low, top_value):
    loudness = 1.0
    for position, shards_of in split:
        heights = jax.random.uniform(jax.random.fold_in(jax.random.fold_in(key, 6), position), (shards_of,), jnp.float32, low / len(split), top_value / len(split))
        loudness = loudness * jnp.repeat(jnp.exp(heights), shape[position] // shards_of).reshape((-1,) + (1,) * (len(shape) - 1 - position))
    return loudness


def normal_values(stream_key, dims, width, most, pieces=(), kind=jnp.bfloat16):
    drawn = jax.random.normal(stream_key, dims, jnp.float32) * width
    if len(pieces) > 0:
        drawn = levels(stream_key, dims, pieces, -0.22, 0.18) * drawn
    return jnp.clip(drawn, min=-most, max=most).astype(kind)


def setup_inputs(seed: int = 0) -> dict:
    splits = jax.random.split(jax.random.key(seed), 8)
    return {
        "residual": normal_values(splits[0], (N_SUB, N_REGION, NOWN, C), 1.0, 6.0, ((0, 16), (1, 32))),
        "send_rows": place_ends(jax.random.randint(splits[1], (N_SUB, N_REGION, 4, OV), 0, NOWN), jax.random.fold_in(splits[1], 1), 0, NOWN - 1).astype(jnp.int32),
        "local_inverse": normal_values(splits[2], (N_SUB, N_REGION, NOWN, SUBN), SUBN ** -0.5, 0.21875, ((0, 16), (1, 32))),
        "coarse_basis": normal_values(splits[3], (N_SUB, N_REGION, NOWN, KC), NOWN ** -0.5, 0.25, ((0, 16), (1, 32))),
        "regional_inverse": normal_values(splits[4], (N_SUB, N_REGION, KC, RC), RC ** -0.5, 0.125, ((0, 16), (1, 32))),
        "root_map": normal_values(splits[5], (N_SUB, N_REGION, KC, KR), KR ** -0.5, 0.75, ((0, 16), (1, 32))),
        "root_inverse": normal_values(splits[6], (N_REGION, KR, ROOT), (ROOT * RC // KR) ** -0.5, 0.0234375, ((0, 32),)),
    }


def pick_rows(res, idx):
    return jnp.take(res, idx, axis=0)


def reference(residual, send_rows, local_inverse, coarse_basis, regional_inverse, root_map, root_inverse):
    idx = send_rows.reshape(N_SUB, N_REGION, 4 * OV).astype(jnp.int32)
    lent = jax.vmap(jax.vmap(pick_rows))(residual, idx).reshape(N_SUB, N_REGION, 4, OV, C)
    zero_sub = jnp.zeros((1, N_REGION, OV, C), residual.dtype)
    zero_reg = jnp.zeros((N_SUB, 1, OV, C), residual.dtype)
    prev_sub = jnp.concatenate([zero_sub, lent[:-1, :, 1]], axis=0)
    next_sub = jnp.concatenate([lent[1:, :, 0], zero_sub], axis=0)
    prev_reg = jnp.concatenate([zero_reg, lent[:, :-1, 3]], axis=1)
    next_reg = jnp.concatenate([lent[:, 1:, 2], zero_reg], axis=1)

    def rhs_one(xs):
        basis, res = xs
        return jnp.einsum('gnk,gnc->gkc', basis.astype(jnp.float32), res.astype(jnp.float32)).astype(jnp.bfloat16)

    coarse_rhs = lax.map(rhs_one, (coarse_basis, residual))
    stacked = coarse_rhs.transpose(1, 0, 2, 3).reshape(N_REGION, RC, C).astype(jnp.float32)

    def regional_one(inv):
        return jnp.einsum('gkr,grc->gkc', inv.astype(jnp.float32), stacked)

    regional = lax.map(regional_one, regional_inverse)
    root_rhs = jnp.einsum('sgkr,sgkc->grc', root_map.astype(jnp.float32), coarse_rhs.astype(jnp.float32)).astype(jnp.bfloat16)
    whole = root_rhs.reshape(ROOT, C).astype(jnp.float32)
    root_sol = jnp.einsum('grq,qc->grc', root_inverse.astype(jnp.float32), whole).astype(jnp.bfloat16)
    weights = (regional + jnp.einsum('sgkr,grc->sgkc', root_map.astype(jnp.float32), root_sol.astype(jnp.float32))).astype(jnp.bfloat16)

    def final_one(xs):
        inv, res, ps, ns, pr, nr, basis, wts = xs
        vec = jnp.concatenate([res, ps, ns, pr, nr], axis=1).astype(jnp.float32)
        local = jnp.einsum('gij,gjc->gic', inv.astype(jnp.float32), vec)
        coarse = jnp.einsum('gnk,gkc->gnc', basis.astype(jnp.float32), wts.astype(jnp.float32))
        return (local + coarse).astype(jnp.bfloat16)

    return lax.map(final_one, (local_inverse, residual, prev_sub, next_sub, prev_reg, next_reg, coarse_basis, weights))
```

```python
import functools

import jax
import jax.numpy as jnp
from jax import lax
from jax.experimental import pallas as pl
from jax.experimental.pallas import tpu as pltpu
from jax.sharding import PartitionSpec as P

F32 = jnp.float32
BF16 = jnp.bfloat16
MESH = pl.DeviceIdType.MESH
NH = 2


def contract_rows(a, b):
    return lax.dot_general(a, b, (((0,), (0,)), ((), ())), preferred_element_type=F32)


def kernel(
    n_sub, n_region,
    res_hbm, rows_hbm, inv_hbm, basis_hbm, reg_hbm, map_hbm, root_hbm, out_hbm,
    res, rows, inv, basis, reginv, rmap, rootinv,
    xbuf, lent, margins, rs_send, rs_recv, gath, sols, regional, local, out,
    in_sem, out_sem, ring_send, ring_recv, share_send, share_recv,
    lent_send, lent_recv, rs_ss, rs_rs, pl_ss, pl_rs, so_ss, so_rs,
):
    s = lax.axis_index("sub")
    g = lax.axis_index("region")
    n_z = n_sub // 2
    z, c = s // 2, s % 2
    sib = s + 1 - 2 * c
    n_cols = res.shape[1]
    kc = basis.shape[1]
    wide = n_cols // NH

    loads = [
        pltpu.make_async_copy(a, b, in_sem.at[i])
        for i, (a, b) in enumerate(
            (
                (basis_hbm, basis), (res_hbm, res), (map_hbm, rmap), (rows_hbm, rows),
                (inv_hbm, inv), (root_hbm, rootinv), (reg_hbm, reginv),
            )
        )
    ]
    for load in loads:
        load.start()

    barrier = pltpu.get_barrier_semaphore()

    @pl.loop(1, n_sub)
    def _(k):
        pl.semaphore_signal(barrier, inc=1, device_id=(lax.rem(s + k, n_sub), g), device_id_type=MESH)

    @pl.loop(1, n_region)
    def _(k):
        pl.semaphore_signal(barrier, inc=1, device_id=(s, lax.rem(g + k, n_region)), device_id_type=MESH)

    core_rows = pl.ds(pl.multiple_of(c * kc, kc), kc)
    loads[0].wait()
    loads[1].wait()
    x = contract_rows(basis[...], res[...]).astype(BF16)
    xbuf[z, core_rows, :] = x

    loads[2].wait()
    proj = contract_rows(rmap[...], x)
    half = proj.shape[0] // 2
    low = lax.broadcasted_iota(jnp.int32, (half, 128), 1) < 64
    for zz in range(n_z):
        top = proj[:half, zz * 128:(zz + 1) * 128]
        bot = proj[half:, zz * 128:(zz + 1) * 128]
        rs_send[2 * zz] = jnp.where(low, top, pltpu.roll(bot, 64, 1))
        rs_send[2 * zz + 1] = jnp.where(low, pltpu.roll(top, 64, 1), bot)

    pl.semaphore_wait(barrier, n_sub - 1 + n_region - 1)

    def rs_copy(k):
        to = lax.rem(s + k, n_sub)
        return pltpu.make_async_remote_copy(
            rs_send.at[to], rs_recv.at[k - 1], rs_ss, rs_rs, device_id=(to, g), device_id_type=MESH
        )

    @pl.loop(1, n_sub)
    def _(k):
        rs_copy(k).start()

    def block(zz, h):
        return xbuf.at[zz, core_rows, pl.ds(h * wide, wide)]

    def ring(way, t, h):
        to = lax.rem(z + (1 if way == 0 else n_z - 1), n_z)
        zz = lax.rem(z + (n_z - t if way == 0 else t), n_z)
        ref = block(zz, h)
        return pltpu.make_async_remote_copy(
            ref, ref, ring_send.at[way, t, h], ring_recv.at[way, t, h],
            device_id=(2 * to + c, g), device_id_type=MESH,
        )

    def ring_arrived(way, t, h):
        zz = lax.rem(z + (n_z - t - 1 if way == 0 else t + 1), n_z)
        ref = block(zz, h)
        pltpu.make_async_copy(ref, ref, ring_recv.at[way, t, h]).wait()

    def share(d, h):
        ref = block(lax.rem(z + d, n_z), h)
        return pltpu.make_async_remote_copy(
            ref, ref, share_send.at[d, h], share_recv.at[d, h],
            device_id=(sib, g), device_id_type=MESH,
        )

    def shared_arrived(d, h):
        zz = lax.rem(z + d, n_z)
        ref = xbuf.at[zz, pl.ds(pl.multiple_of((1 - c) * kc, kc), kc), pl.ds(h * wide, wide)]
        pltpu.make_async_copy(ref, ref, share_recv.at[d, h]).wait()

    last = n_z // 2 - 1

    def goes(way, t, h):
        return t < last or (t == last and (h < NH // 2) == (way == 0))

    for h in range(NH):
        for way in range(2):
            ring(way, 0, h).start()
    for h in range(NH):
        share(0, h).start()

    loads[3].wait()
    owned = res.shape[0]
    margin = rows.shape[1]

    def lent_copy(j):
        to = ((s - 1, g), (s + 1, g), (s, g - 1), (s, g + 1))[j]
        place = (1, 0, 3, 2)[j]
        return pltpu.make_async_remote_copy(
            lent.at[pl.ds(j * margin, margin)], margins.at[pl.ds(place * margin, margin)],
            lent_send.at[j], lent_recv.at[place], device_id=to, device_id_type=MESH,
        )

    has = (s > 0, s < n_sub - 1, g > 0, g < n_region - 1)
    for j in range(4):
        row_id = lax.broadcasted_iota(jnp.int32, (owned, margin), 0)
        pick = jnp.where(row_id == rows[pl.ds(j, 1), :], 1.0, 0.0).astype(BF16)
        lent[pl.ds(j * margin, margin), :] = contract_rows(pick, res[...]).astype(BF16)

        @pl.when(has[j])
        def _():
            lent_copy(j).start()

        @pl.when(jnp.logical_not(has[j]))
        def _():
            margins[pl.ds(j * margin, margin), :] = jnp.zeros((margin, n_cols), BF16)

    pltpu.make_async_copy(rs_recv, rs_recv, rs_rs).wait()
    total = rs_send[s] + rs_recv[0]
    for k in range(1, n_sub - 1):
        total += rs_recv[k]
    gath[g] = total.astype(BF16)

    def plane_copy(k):
        to = lax.rem(g + k, n_region)
        return pltpu.make_async_remote_copy(
            gath.at[g], gath.at[g], pl_ss, pl_rs, device_id=(s, to), device_id_type=MESH
        )

    @pl.loop(1, n_region)
    def _(k):
        plane_copy(k).start()

    def step(t):
        for h in range(NH):
            for way in range(2):
                if goes(way, t, h):
                    ring_arrived(way, t, h)
                    if t < last and goes(way, t + 1, h):
                        ring(way, t + 1, h).start()
                    share(n_z - t - 1 if way == 0 else t + 1, h).start()

    def regional_block(d, first=False):
        zz = lax.rem(z + d, n_z)
        for h in range(NH):
            shared_arrived(d, h)
        part = jnp.dot(
            reginv[:, pl.ds(pl.multiple_of(zz * 2 * kc, 2 * kc), 2 * kc)], xbuf[zz],
            preferred_element_type=F32,
        )
        regional[...] = part if first else regional[...] + part

    step(0)
    loads[4].wait()
    local[...] = jnp.dot(inv[:, :owned], res[...], preferred_element_type=F32)
    loads[6].wait()
    regional_block(0, True)
    step(1)
    regional_block(1)
    regional_block(n_z - 1)

    loads[5].wait()
    others = gath.at[pl.ds(0, n_region - 1)]
    pltpu.make_async_copy(others, others, pl_rs).wait()
    packed = gath[...]
    lowb = lax.broadcasted_iota(jnp.int32, packed.shape, 2) < 64
    zero = jnp.zeros_like(packed)
    both = jnp.concatenate([jnp.where(lowb, packed, zero), jnp.where(lowb, zero, packed)], axis=1)
    sol = jnp.dot(rootinv[...], both.reshape(2 * half * n_region, 128), preferred_element_type=F32)
    sol = sol + pltpu.roll(sol, 64, 1)
    sols[s] = jnp.where(low, sol[:half], sol[half:]).astype(BF16)

    def sol_copy(k):
        to = lax.rem(s + k, n_sub)
        return pltpu.make_async_remote_copy(
            sols.at[s], sols.at[s], so_ss, so_rs, device_id=(to, g), device_id_type=MESH
        )

    @pl.loop(1, n_sub)
    def _(k):
        sol_copy(k).start()

    step(2)

    for j in range(4):
        @pl.when(has[j])
        def _():
            ref = margins.at[pl.ds(j * margin, margin)]
            pltpu.make_async_copy(ref, ref, lent_recv.at[j]).wait()

    local[...] += jnp.dot(inv[:, owned:], margins[...], preferred_element_type=F32)
    for d in (2, n_z - 2, 3, n_z - 3):
        regional_block(d)

    others_sol = sols.at[pl.ds(0, n_sub - 1)]
    pltpu.make_async_copy(others_sol, others_sol, so_rs).wait()
    for zz in range(n_z):
        p0 = sols[2 * zz].astype(F32)
        p1 = sols[2 * zz + 1].astype(F32)
        top = jnp.where(low, p0, pltpu.roll(p1, 64, 1))
        bot = jnp.where(low, pltpu.roll(p0, 64, 1), p1)
        rsol = jnp.concatenate([top, bot], axis=0).astype(BF16)
        cols = slice(zz * 128, (zz + 1) * 128)
        regional[:, cols] += jnp.dot(rmap[...], rsol, preferred_element_type=F32)

    step(3)
    regional_block(n_z // 2)

    n_out = 4
    stores = []
    for n in range(n_out):
        width = n_cols // n_out
        cols = slice(n * width, (n + 1) * width)
        w = regional[:, cols].astype(BF16)
        out[:, cols] = (
            local[:, cols] + jnp.dot(basis[...], w, preferred_element_type=F32)
        ).astype(BF16)
        store = pltpu.make_async_copy(
            out.at[:, pl.ds(n * width, width)], out_hbm.at[:, pl.ds(n * width, width)], out_sem.at[n]
        )
        store.start()
        stores.append(store)

    for h in range(NH):
        for way in range(2):
            for t in range(last + 1):
                if goes(way, t, h):
                    ring(way, t, h).wait_send()
        for d in range(n_z):
            share(d, h).wait_send()
    for j in range(4):
        @pl.when(has[j])
        def _():
            lent_copy(j).wait_send()
    pltpu.make_async_copy(rs_recv, rs_recv, rs_ss).wait()
    pltpu.make_async_copy(others, others, pl_ss).wait()
    pltpu.make_async_copy(others_sol, others_sol, so_ss).wait()
    for store in stores:
        store.wait()


def per_device(n_sub, n_region, residual, send_rows, local_inverse, coarse_basis, regional_inverse, root_map, root_inverse):
    args = (
        residual[0, 0], send_rows[0, 0], local_inverse[0, 0], coarse_basis[0, 0],
        regional_inverse[0, 0], root_map[0, 0], root_inverse[0],
    )
    res, rows, inv, basis, reginv, rmap, rootinv = args
    owned, cols = res.shape
    kc, kr = rmap.shape
    margin = rows.shape[1]
    n_z = n_sub // 2
    dma = pltpu.SemaphoreType.DMA
    flops = 2 * cols * (owned * inv.shape[1] + kc * reginv.shape[1] + 2 * kc * owned + 4 * kr * kc + 4 * margin * owned)
    out = pl.pallas_call(
        functools.partial(kernel, n_sub, n_region),
        out_shape=jax.ShapeDtypeStruct((owned, cols), BF16),
        in_specs=[pl.BlockSpec(memory_space=pl.ANY)] * 7,
        out_specs=pl.BlockSpec(memory_space=pl.ANY),
        scratch_shapes=[pltpu.VMEM(a.shape, a.dtype) for a in args]
        + [
            pltpu.VMEM((n_z, 2 * kc, cols), BF16),
            pltpu.VMEM((4 * margin, cols), BF16),
            pltpu.VMEM((4 * margin, cols), BF16),
            pltpu.VMEM((n_sub, kr // 2, 128), F32),
            pltpu.VMEM((n_sub - 1, kr // 2, 128), F32),
            pltpu.VMEM((n_region, kr // 2, 128), BF16),
            pltpu.VMEM((n_sub, kr // 2, 128), BF16),
            pltpu.VMEM((kc, cols), F32),
            pltpu.VMEM((owned, cols), F32),
            pltpu.VMEM((owned, cols), BF16),
            dma((7,)), dma((4,)),
            dma((2, n_z // 2, NH)), dma((2, n_z // 2, NH)),
            dma((n_z, NH)), dma((n_z, NH)),
            dma((4,)), dma((4,)),
            dma, dma, dma, dma, dma, dma,
        ],
        compiler_params=pltpu.CompilerParams(
            collective_id=0, has_side_effects=True, vmem_limit_bytes=48 * 1024 * 1024
        ),
        cost_estimate=pl.CostEstimate(flops=flops, bytes_accessed=4 << 20, transcendentals=0),
    )(*args)
    return out.reshape(1, 1, owned, cols)


def solution(mesh):
    here = P("sub", "region", None, None)
    return jax.shard_map(
        functools.partial(per_device, mesh.shape["sub"], mesh.shape["region"]),
        mesh=mesh,
        in_specs=(here,) * 6 + (P("region", None, None),),
        out_specs=here,
        check_vma=False,
    )
```

```python
import functools

import jax
import jax.numpy as jnp
from jax import lax
from jax.experimental import pallas as pl
from jax.experimental.pallas import tpu as pltpu
from jax.sharding import PartitionSpec as P

F32 = jnp.float32
BF16 = jnp.bfloat16
MESH = pl.DeviceIdType.MESH
NH = 2
NX = 4


def contract_rows(a, b):
    return lax.dot_general(a, b, (((0,), (0,)), ((), ())), preferred_element_type=F32)


def kernel(
    n_sub, n_region,
    res_hbm, rows_hbm, inv_hbm, basis_hbm, reg_hbm, map_hbm, root_hbm, out_hbm,
    res, rows, inv, basis, reginv, rmap, rootinv,
    xbuf, lent, margins, rs_part, rs_pair, rs_chip, rs_send, rs_recv, gath, sols, regional, local, out,
    in_sem, out_sem, ring_send, ring_recv, share_send, share_recv,
    lent_send, lent_recv, rs_ss, rs_rs, py_ss, py_rs, px_ss, px_rs, so_ss, so_rs,
    pair_sem, ready_near, ready_col, ready_plane,
):
    s = lax.axis_index("sub")
    g = lax.axis_index("region")
    n_z = n_sub // 2
    n_y = n_region // NX
    z, c = s // 2, s % 2
    y, xx = g // NX, g % NX
    sib = s + 1 - 2 * c
    n_cols = res.shape[1]
    kc = basis.shape[1]
    wide = n_cols // NH
    margin = rows.shape[1]
    owned = res.shape[0]

    def piece(ref, h):
        return ref.at[:, pl.ds(h * wide, wide)]

    basis_load = pltpu.make_async_copy(basis_hbm, basis, in_sem.at[0])
    res_loads = [pltpu.make_async_copy(piece(res_hbm, h), piece(res, h), in_sem.at[1 + h]) for h in range(NH)]
    map_load, rows_load, inv_load, reg_load, root_load = [
        pltpu.make_async_copy(a, b, in_sem.at[1 + NH + i])
        for i, (a, b) in enumerate(
            ((map_hbm, rmap), (rows_hbm, rows), (inv_hbm, inv), (reg_hbm, reginv), (root_hbm, rootinv))
        )
    ]
    for load in (basis_load, *res_loads, map_load, rows_load, inv_load, reg_load, root_load):
        load.start()

    barrier = pltpu.get_barrier_semaphore()

    def signal(sem, to):
        pl.semaphore_signal(sem, inc=1, device_id=to, device_id_type=MESH)

    def wait_for(sem, n):
        pl.when(n > 0)(lambda: pl.semaphore_wait(sem, n))

    def y_rank(v):
        far = jnp.minimum(v, n_y - v)
        return jnp.where(v == 0, 0, 2 * far - 1 + jnp.where(v > n_y // 2, 1, 0))

    my_rank = y_rank(y)
    before_far = jnp.logical_and(xx == 0, y > 0)
    after_far = jnp.logical_and(xx == NX - 1, y < n_y - 1)
    plane = [((s, v * NX + xx), y != v, y_rank(v) > my_rank) for v in range(n_y)]
    plane += [((s, y * NX + v), xx != v, xx < v) for v in range(NX)]
    plane += [
        ((s, g - 1), before_far, y_rank(y - 1) > my_rank),
        ((s, g + 1), after_far, y_rank(y + 1) > my_rank),
    ]
    higher = [jnp.logical_and(there, up) for _, there, up in plane]
    lower = [jnp.logical_and(there, jnp.logical_not(up)) for _, there, up in plane]

    def count(flags):
        return sum(jnp.where(f, 1, 0) for f in flags)

    @pl.loop(z + 1, n_z)
    def _(to):
        signal(barrier, (2 * to + c, g))

    pl.when(c == 0)(lambda: signal(barrier, (sib, g)))
    across_down = jnp.logical_and(c == 0, z > 0)
    across_up = jnp.logical_and(c == 1, z < n_z - 1)
    pl.when(across_up)(lambda: signal(barrier, (s + 1, g)))

    for (to, _, _), up in zip(plane, higher):
        @pl.when(up)
        def _():
            signal(barrier, to)

    wait_for(barrier, z + c + count([across_down, *lower]))

    pl.when(z > 0)(lambda: signal(ready_near, (s - 2, g)))
    pl.when(c == 1)(lambda: signal(ready_near, (sib, g)))

    @pl.loop(0, z - 1)
    def _(to):
        signal(ready_col, (2 * to + c, g))

    pl.when(across_down)(lambda: signal(ready_col, (s - 1, g)))

    for (to, _, _), low_one in zip(plane, lower):
        @pl.when(low_one)
        def _():
            signal(ready_plane, to)

    n_near = count([z < n_z - 1, c == 0])
    n_far = jnp.maximum(n_z - 2 - z, 0) + count([across_up])

    core_rows = pl.ds(pl.multiple_of(c * kc, kc), kc)

    def block(zz, h):
        return xbuf.at[zz, core_rows, pl.ds(h * wide, wide)]

    def ring(way, t, h):
        to = lax.rem(z + (1 if way == 0 else n_z - 1), n_z)
        zz = lax.rem(z + (n_z - t if way == 0 else t), n_z)
        ref = block(zz, h)
        return pltpu.make_async_remote_copy(
            ref, ref, ring_send.at[way, t, h], ring_recv.at[way, t, h],
            device_id=(2 * to + c, g), device_id_type=MESH,
        )

    def ring_arrived(way, t, h):
        zz = lax.rem(z + (n_z - t - 1 if way == 0 else t + 1), n_z)
        ref = block(zz, h)
        pltpu.make_async_copy(ref, ref, ring_recv.at[way, t, h]).wait()

    def share(d, h):
        ref = block(lax.rem(z + d, n_z), h)
        return pltpu.make_async_remote_copy(
            ref, ref, share_send.at[d, h], share_recv.at[d, h],
            device_id=(sib, g), device_id_type=MESH,
        )

    def shared_arrived(d, h):
        zz = lax.rem(z + d, n_z)
        ref = xbuf.at[zz, pl.ds(pl.multiple_of((1 - c) * kc, kc), kc), pl.ds(h * wide, wide)]
        pltpu.make_async_copy(ref, ref, share_recv.at[d, h]).wait()

    last = n_z // 2 - 1

    def takes(way, t, h, to):
        if t < last:
            return None
        if (h < NH // 2) == (way == 0):
            return None if way == 1 else to != 0
        return to == 0 if way == 1 else False

    def when(cond, then):
        if cond is None:
            then()
        elif cond is not False:
            pl.when(cond)(then)

    chip_to = (lax.rem(z + 1, n_z), lax.rem(z + n_z - 1, n_z))

    basis_load.wait()
    for h in range(NH):
        res_loads[h].wait()
        cols = slice(h * wide, (h + 1) * wide)
        xbuf[z, core_rows, cols] = contract_rows(basis[...], res[:, cols]).astype(BF16)
        if h == 0:
            wait_for(ready_near, n_near)
            ring(0, 0, 0).start()
            pl.when(z > 0)(lambda: ring(1, 0, 0).start())
        share(0, h).start()

    map_load.wait()
    proj = jnp.dot(rmap[...], xbuf[z, core_rows, :], preferred_element_type=F32)
    half = proj.shape[0] // 2
    low = lax.broadcasted_iota(jnp.int32, (half, 128), 1) < 64
    for zz in range(n_z):
        top = proj[:half, zz * 128:(zz + 1) * 128]
        bot = proj[half:, zz * 128:(zz + 1) * 128]
        rs_part[0, zz] = jnp.where(low, top, pltpu.roll(bot, 64, 1))
        rs_part[1, zz] = jnp.where(low, pltpu.roll(top, 64, 1), bot)

    pair = pltpu.make_async_remote_copy(
        rs_part.at[1 - c], rs_pair, pair_sem.at[0], pair_sem.at[1], device_id=(sib, g), device_id_type=MESH
    )
    pair.start()
    pair.wait_recv()
    rs_chip[...] = rs_part[c] + rs_pair[...]
    rs_send[...] = rs_chip[...].astype(BF16)

    def rs_copy(to):
        return pltpu.make_async_remote_copy(
            rs_send.at[to], rs_recv.at[lax.rem(to - z + n_z, n_z) - 1], rs_ss, rs_rs,
            device_id=(2 * to + c, g), device_id_type=MESH,
        )

    @pl.loop(0, z)
    def _(to):
        rs_copy(to).start()

    def follow(way):
        for h in range(1, NH):
            ring(way, 0, h - 1).wait_send()
            ring(way, 0, h).start()

    follow(0)
    pl.when(z > 0)(lambda: follow(1))
    wait_for(ready_col, n_far)

    @pl.when(z == 0)
    def _():
        ring(1, 0, 0).start()

    @pl.loop(z + 1, n_z)
    def _(to):
        rs_copy(to).start()

    rows_load.wait()

    def lent_copy(j):
        to = ((s - 1, g), (s + 1, g), (s, g - 1), (s, g + 1))[j]
        place = (1, 0, 3, 2)[j]
        return pltpu.make_async_remote_copy(
            lent.at[pl.ds(j * margin, margin)], margins.at[pl.ds(place * margin, margin)],
            lent_send.at[j], lent_recv.at[place], device_id=to, device_id_type=MESH,
        )

    has = (s > 0, s < n_sub - 1, g > 0, g < n_region - 1)
    for j in range(4):
        if j == 2:
            wait_for(ready_plane, count(higher))
        row_id = lax.broadcasted_iota(jnp.int32, (owned, margin), 0)
        pick = jnp.where(row_id == rows[pl.ds(j, 1), :], 1.0, 0.0).astype(BF16)
        lent[pl.ds(j * margin, margin), :] = contract_rows(pick, res[...]).astype(BF16)

        @pl.when(has[j])
        def _():
            lent_copy(j).start()

        @pl.when(jnp.logical_not(has[j]))
        def _():
            margins[pl.ds(j * margin, margin), :] = jnp.zeros((margin, n_cols), BF16)

    pl.when(z == 0)(lambda: follow(1))

    inv_load.wait()
    local[...] = jnp.dot(inv[:, :owned], res[...], preferred_element_type=F32)

    def step(t, pieces=range(NH)):
        for h in pieces:
            for way in range(2):
                def arrived():
                    ring_arrived(way, t, h)
                    if t < last:
                        when(takes(way, t + 1, h, chip_to[way]), lambda: ring(way, t + 1, h).start())
                    share(n_z - t - 1 if way == 0 else t + 1, h).start()

                when(takes(way, t, h, z), arrived)

    def regional_block(d, first=False):
        zz = lax.rem(z + d, n_z)
        for h in range(NH):
            shared_arrived(d, h)
        part = jnp.dot(
            reginv[:, pl.ds(pl.multiple_of(zz * 2 * kc, 2 * kc), 2 * kc)], xbuf[zz],
            preferred_element_type=F32,
        )
        regional[...] = part if first else regional[...] + part

    reg_load.wait()
    regional_block(0, True)
    step(0)

    pltpu.make_async_copy(rs_recv, rs_recv, rs_rs).wait()
    total = rs_chip[z]
    for k in range(n_z - 1):
        total += rs_recv[k].astype(F32)
    gath[xx, y] = total.astype(BF16)

    def y_copy(k):
        to = lax.rem(y + k, n_y)
        return pltpu.make_async_remote_copy(
            gath.at[xx, y], gath.at[xx, y], py_ss, py_rs, device_id=(s, to * NX + xx), device_id_type=MESH
        )

    def x_copy(k):
        to = lax.rem(xx + k, NX)
        return pltpu.make_async_remote_copy(
            gath.at[xx], gath.at[xx], px_ss, px_rs, device_id=(s, y * NX + to), device_id_type=MESH
        )

    for k in range(1, n_y):
        y_copy(k).start()

    regional_block(1)
    regional_block(n_z - 1)
    step(1, range(NH // 2))

    others_y = gath.at[0, pl.ds(0, n_y - 1)]
    pltpu.make_async_copy(others_y, others_y, py_rs).wait()
    for k in range(1, NX):
        x_copy(k).start()

    step(1, range(NH // 2, NH))
    regional_block(2)
    regional_block(n_z - 2)

    root_load.wait()
    others_x = gath.at[pl.ds(0, NX - 1)]
    pltpu.make_async_copy(others_x, others_x, px_rs).wait()
    zero = jnp.zeros((half, 128), BF16)
    lowb = lax.broadcasted_iota(jnp.int32, (half, 128), 1) < 64
    both = []
    for v in range(n_y):
        for u in range(NX):
            packed = gath[u, v]
            both += [jnp.where(lowb, packed, zero), jnp.where(lowb, zero, packed)]
    sol = jnp.dot(rootinv[...], jnp.concatenate(both, axis=0), preferred_element_type=F32)
    sol = sol + pltpu.roll(sol, 64, 1)
    sols[c, z] = jnp.where(low, sol[:half], sol[half:]).astype(BF16)

    def sol_copy(k):
        to = lax.rem(z + k, n_z)
        return pltpu.make_async_remote_copy(
            sols.at[c, z], sols.at[c, z], so_ss, so_rs, device_id=(2 * to + c, g), device_id_type=MESH
        )

    @pl.loop(1, n_z)
    def _(k):
        sol_copy(k).start()

    step(2)

    for j in range(4):
        @pl.when(has[j])
        def _():
            ref = margins.at[pl.ds(j * margin, margin)]
            pltpu.make_async_copy(ref, ref, lent_recv.at[j]).wait()

    local[...] += jnp.dot(inv[:, owned:], margins[...], preferred_element_type=F32)
    for d in (3, n_z - 3):
        regional_block(d)

    others_sol = sols.at[0, pl.ds(0, n_z - 1)]
    pltpu.make_async_copy(others_sol, others_sol, so_rs).wait()
    sol_pair = pltpu.make_async_remote_copy(
        sols.at[c], sols.at[c], pair_sem.at[2], pair_sem.at[3], device_id=(sib, g), device_id_type=MESH
    )
    sol_pair.start()
    other_core = sols.at[1 - c]
    pltpu.make_async_copy(other_core, other_core, pair_sem.at[3]).wait()
    for zz in range(n_z):
        p0 = sols[0, zz].astype(F32)
        p1 = sols[1, zz].astype(F32)
        top = jnp.where(low, p0, pltpu.roll(p1, 64, 1))
        bot = jnp.where(low, pltpu.roll(p0, 64, 1), p1)
        rsol = jnp.concatenate([top, bot], axis=0).astype(BF16)
        cols = slice(zz * 128, (zz + 1) * 128)
        regional[:, cols] += contract_rows(rmap[...], rsol)

    step(3)
    regional_block(n_z // 2)

    n_out = 4
    stores = []
    for n in range(n_out):
        width = n_cols // n_out
        cols = slice(n * width, (n + 1) * width)
        w = regional[:, cols].astype(BF16)
        out[:, cols] = (
            local[:, cols] + jnp.dot(basis[...], w, preferred_element_type=F32)
        ).astype(BF16)
        store = pltpu.make_async_copy(
            out.at[:, pl.ds(n * width, width)], out_hbm.at[:, pl.ds(n * width, width)], out_sem.at[n]
        )
        store.start()
        stores.append(store)

    for h in range(NH):
        for way in range(2):
            for t in range(last + 1):
                if t > 0 or h == NH - 1:
                    when(takes(way, t, h, chip_to[way]), lambda: ring(way, t, h).wait_send())
        for d in range(n_z):
            share(d, h).wait_send()
    for j in range(4):
        @pl.when(has[j])
        def _():
            lent_copy(j).wait_send()
    pltpu.make_async_copy(rs_recv, rs_recv, rs_ss).wait()
    pair.wait_send()
    sol_pair.wait_send()
    pltpu.make_async_copy(others_y, others_y, py_ss).wait()
    pltpu.make_async_copy(others_x, others_x, px_ss).wait()
    pltpu.make_async_copy(others_sol, others_sol, so_ss).wait()
    for store in stores:
        store.wait()


def per_device(n_sub, n_region, residual, send_rows, local_inverse, coarse_basis, regional_inverse, root_map, root_inverse):
    args = (
        residual[0, 0], send_rows[0, 0], local_inverse[0, 0], coarse_basis[0, 0],
        regional_inverse[0, 0], root_map[0, 0].T, root_inverse[0],
    )
    res, rows, inv, basis, reginv, rmap, rootinv = args
    owned, cols = res.shape
    kr, kc = rmap.shape
    margin = rows.shape[1]
    n_z = n_sub // 2
    dma = pltpu.SemaphoreType.DMA
    flops = 2 * cols * (owned * inv.shape[1] + kc * reginv.shape[1] + 2 * kc * owned + 4 * kr * kc + 4 * margin * owned)
    out = pl.pallas_call(
        functools.partial(kernel, n_sub, n_region),
        out_shape=jax.ShapeDtypeStruct((owned, cols), BF16),
        in_specs=[pl.BlockSpec(memory_space=pl.ANY)] * 7,
        out_specs=pl.BlockSpec(memory_space=pl.ANY),
        scratch_shapes=[pltpu.VMEM(a.shape, a.dtype) for a in args]
        + [
            pltpu.VMEM((n_z, 2 * kc, cols), BF16),
            pltpu.VMEM((4 * margin, cols), BF16),
            pltpu.VMEM((4 * margin, cols), BF16),
            pltpu.VMEM((2, n_z, kr // 2, 128), F32),
            pltpu.VMEM((n_z, kr // 2, 128), F32),
            pltpu.VMEM((n_z, kr // 2, 128), F32),
            pltpu.VMEM((n_z, kr // 2, 128), BF16),
            pltpu.VMEM((n_z - 1, kr // 2, 128), BF16),
            pltpu.VMEM((NX, n_region // NX, kr // 2, 128), BF16),
            pltpu.VMEM((2, n_z, kr // 2, 128), BF16),
            pltpu.VMEM((kc, cols), F32),
            pltpu.VMEM((owned, cols), F32),
            pltpu.VMEM((owned, cols), BF16),
            dma((6 + NH,)), dma((4,)),
            dma((2, n_z // 2, NH)), dma((2, n_z // 2, NH)),
            dma((n_z, NH)), dma((n_z, NH)),
            dma((4,)), dma((4,)),
            *[dma] * 8,
            dma((4,)),
            *[pltpu.SemaphoreType.REGULAR] * 3,
        ],
        compiler_params=pltpu.CompilerParams(
            collective_id=0, has_side_effects=True, vmem_limit_bytes=60 * 1024 * 1024
        ),
        cost_estimate=pl.CostEstimate(flops=flops, bytes_accessed=4 << 20, transcendentals=0),
    )(*args)
    return out.reshape(1, 1, owned, cols)


def solution(mesh):
    here = P("sub", "region", None, None)
    return jax.shard_map(
        functools.partial(per_device, mesh.shape["sub"], mesh.shape["region"]),
        mesh=mesh,
        in_specs=(here,) * 6 + (P("region", None, None),),
        out_specs=here,
        check_vma=False,
    )
```

```python
import functools

import jax
import jax.numpy as jnp
from jax import lax
from jax.experimental import pallas as pl
from jax.experimental.pallas import tpu as pltpu
from jax.sharding import PartitionSpec as P

F32 = jnp.float32
BF16 = jnp.bfloat16
MESH = pl.DeviceIdType.MESH
NH = 2
NX = 4


def contract_rows(a, b):
    return lax.dot_general(a, b, (((0,), (0,)), ((), ())), preferred_element_type=F32)


def kernel(
    n_sub, n_region,
    res_hbm, rows_hbm, inv_hbm, basis_hbm, reg_hbm, map_hbm, root_hbm, out_hbm,
    res, rows, inv, basis, reginv, rmap, rootinv,
    xbuf, lent, margins, rs_part, rs_pair, rs_chip, rs_send, rs_recv, gath, sols, regional, local, out,
    in_sem, out_sem, ring_send, ring_recv, share_send, share_recv,
    lent_send, lent_recv, rs_ss, rs_rs, py_ss, py_rs, px_ss, px_rs, so_ss, so_rs,
    pair_sem, ready_near, ready_col, ready_plane,
):
    s = lax.axis_index("sub")
    g = lax.axis_index("region")
    n_z = n_sub // 2
    n_y = n_region // NX
    z, c = s // 2, s % 2
    y, xx = g // NX, g % NX
    sib = s + 1 - 2 * c
    n_cols = res.shape[1]
    kc = basis.shape[1]
    wide = n_cols // NH
    margin = rows.shape[1]
    owned = res.shape[0]

    def piece(ref, h):
        return ref.at[:, pl.ds(h * wide, wide)]

    basis_load = pltpu.make_async_copy(basis_hbm, basis, in_sem.at[0])
    res_loads = [pltpu.make_async_copy(piece(res_hbm, h), piece(res, h), in_sem.at[1 + h]) for h in range(NH)]
    map_load, rows_load, inv_load, reg_load, root_load = [
        pltpu.make_async_copy(a, b, in_sem.at[1 + NH + i])
        for i, (a, b) in enumerate(
            ((map_hbm, rmap), (rows_hbm, rows), (inv_hbm, inv), (reg_hbm, reginv), (root_hbm, rootinv))
        )
    ]
    for load in (basis_load, *res_loads, map_load, rows_load, inv_load, reg_load, root_load):
        load.start()

    barrier = pltpu.get_barrier_semaphore()

    def signal(sem, to):
        pl.semaphore_signal(sem, inc=1, device_id=to, device_id_type=MESH)

    def wait_for(sem, n):
        pl.when(n > 0)(lambda: pl.semaphore_wait(sem, n))

    def y_rank(v):
        far = jnp.minimum(v, n_y - v)
        return jnp.where(v == 0, 0, 2 * far - 1 + jnp.where(v > n_y // 2, 1, 0))

    my_rank = y_rank(y)
    before_far = jnp.logical_and(xx == 0, y > 0)
    after_far = jnp.logical_and(xx == NX - 1, y < n_y - 1)
    plane = [((s, v * NX + xx), y != v, y_rank(v) > my_rank) for v in range(n_y)]
    plane += [((s, y * NX + v), xx != v, xx < v) for v in range(NX)]
    plane += [
        ((s, g - 1), before_far, y_rank(y - 1) > my_rank),
        ((s, g + 1), after_far, y_rank(y + 1) > my_rank),
    ]
    higher = [jnp.logical_and(there, up) for _, there, up in plane]
    lower = [jnp.logical_and(there, jnp.logical_not(up)) for _, there, up in plane]

    def count(flags):
        return sum(jnp.where(f, 1, 0) for f in flags)

    @pl.loop(z + 1, n_z)
    def _(to):
        signal(barrier, (2 * to + c, g))

    pl.when(c == 0)(lambda: signal(barrier, (sib, g)))
    across_down = jnp.logical_and(c == 0, z > 0)
    across_up = jnp.logical_and(c == 1, z < n_z - 1)
    pl.when(across_up)(lambda: signal(barrier, (s + 1, g)))

    for (to, _, _), up in zip(plane, higher):
        @pl.when(up)
        def _():
            signal(barrier, to)

    wait_for(barrier, z + c + count([across_down, *lower]))

    pl.when(z > 0)(lambda: signal(ready_near, (s - 2, g)))
    pl.when(c == 1)(lambda: signal(ready_near, (sib, g)))

    @pl.loop(0, z - 1)
    def _(to):
        signal(ready_col, (2 * to + c, g))

    pl.when(across_down)(lambda: signal(ready_col, (s - 1, g)))

    for (to, _, _), low_one in zip(plane, lower):
        @pl.when(low_one)
        def _():
            signal(ready_plane, to)

    n_near = count([z < n_z - 1, c == 0])
    n_far = jnp.maximum(n_z - 2 - z, 0) + count([across_up])

    core_rows = pl.ds(pl.multiple_of(c * kc, kc), kc)

    def block(zz, h):
        return xbuf.at[zz, core_rows, pl.ds(h * wide, wide)]

    def ring(way, t, h):
        to = lax.rem(z + (1 if way == 0 else n_z - 1), n_z)
        zz = lax.rem(z + (n_z - t if way == 0 else t), n_z)
        ref = block(zz, h)
        return pltpu.make_async_remote_copy(
            ref, ref, ring_send.at[way, t, h], ring_recv.at[way, t, h],
            device_id=(2 * to + c, g), device_id_type=MESH,
        )

    def ring_arrived(way, t, h):
        zz = lax.rem(z + (n_z - t - 1 if way == 0 else t + 1), n_z)
        ref = block(zz, h)
        pltpu.make_async_copy(ref, ref, ring_recv.at[way, t, h]).wait()

    def share(d, h):
        ref = block(lax.rem(z + d, n_z), h)
        return pltpu.make_async_remote_copy(
            ref, ref, share_send.at[d, h], share_recv.at[d, h],
            device_id=(sib, g), device_id_type=MESH,
        )

    def shared_arrived(d, h):
        zz = lax.rem(z + d, n_z)
        ref = xbuf.at[zz, pl.ds(pl.multiple_of((1 - c) * kc, kc), kc), pl.ds(h * wide, wide)]
        pltpu.make_async_copy(ref, ref, share_recv.at[d, h]).wait()

    last = n_z // 2 - 1

    def takes(way, t, h, to):
        if t < last:
            return None
        if (h < NH // 2) == (way == 0):
            return None if way == 1 else to != 0
        return to == 0 if way == 1 else False

    def when(cond, then):
        if cond is None:
            then()
        elif cond is not False:
            pl.when(cond)(then)

    chip_to = (lax.rem(z + 1, n_z), lax.rem(z + n_z - 1, n_z))

    basis_load.wait()
    for h in range(NH):
        res_loads[h].wait()
        cols = slice(h * wide, (h + 1) * wide)
        xbuf[z, core_rows, cols] = contract_rows(basis[...], res[:, cols]).astype(BF16)
        if h == 0:
            wait_for(ready_near, n_near)
            ring(0, 0, 0).start()
            pl.when(z > 0)(lambda: ring(1, 0, 0).start())
        share(0, h).start()

    map_load.wait()
    proj = jnp.dot(rmap[...], xbuf[z, core_rows, :], preferred_element_type=F32)
    half = proj.shape[0] // 2
    low = lax.broadcasted_iota(jnp.int32, (half, 128), 1) < 64
    for zz in range(n_z):
        top = proj[:half, zz * 128:(zz + 1) * 128]
        bot = proj[half:, zz * 128:(zz + 1) * 128]
        rs_part[0, zz] = jnp.where(low, top, pltpu.roll(bot, 64, 1))
        rs_part[1, zz] = jnp.where(low, pltpu.roll(top, 64, 1), bot)

    pair = pltpu.make_async_remote_copy(
        rs_part.at[1 - c], rs_pair, pair_sem.at[0], pair_sem.at[1], device_id=(sib, g), device_id_type=MESH
    )
    pair.start()
    pair.wait_recv()
    rs_chip[...] = rs_part[c] + rs_pair[...]
    rs_send[...] = rs_chip[...].astype(BF16)

    def rs_copy(to):
        return pltpu.make_async_remote_copy(
            rs_send.at[to], rs_recv.at[lax.rem(to - z + n_z, n_z) - 1], rs_ss, rs_rs,
            device_id=(2 * to + c, g), device_id_type=MESH,
        )

    @pl.loop(0, z)
    def _(to):
        rs_copy(to).start()

    def follow(way):
        for h in range(1, NH):
            ring(way, 0, h - 1).wait_send()
            ring(way, 0, h).start()

    follow(0)
    pl.when(z > 0)(lambda: follow(1))
    wait_for(ready_col, n_far)

    @pl.when(z == 0)
    def _():
        ring(1, 0, 0).start()

    @pl.loop(z + 1, n_z)
    def _(to):
        rs_copy(to).start()

    rows_load.wait()

    def lent_copy(j):
        to = ((s - 1, g), (s + 1, g), (s, g - 1), (s, g + 1))[j]
        place = (1, 0, 3, 2)[j]
        return pltpu.make_async_remote_copy(
            lent.at[pl.ds(j * margin, margin)], margins.at[pl.ds(place * margin, margin)],
            lent_send.at[j], lent_recv.at[place], device_id=to, device_id_type=MESH,
        )

    has = (s > 0, s < n_sub - 1, g > 0, g < n_region - 1)
    for j in range(4):
        if j == 2:
            wait_for(ready_plane, count(higher))
        row_id = lax.broadcasted_iota(jnp.int32, (owned, margin), 0)
        pick = jnp.where(row_id == rows[pl.ds(j, 1), :], 1.0, 0.0).astype(BF16)
        lent[pl.ds(j * margin, margin), :] = contract_rows(pick, res[...]).astype(BF16)

        @pl.when(has[j])
        def _():
            lent_copy(j).start()

        @pl.when(jnp.logical_not(has[j]))
        def _():
            margins[pl.ds(j * margin, margin), :] = jnp.zeros((margin, n_cols), BF16)

    pl.when(z == 0)(lambda: follow(1))

    inv_load.wait()
    local[...] = jnp.dot(inv[:, :owned], res[...], preferred_element_type=F32)

    def step(t, pieces=range(NH)):
        for h in pieces:
            for way in range(2):
                def arrived():
                    ring_arrived(way, t, h)
                    if t < last:
                        when(takes(way, t + 1, h, chip_to[way]), lambda: ring(way, t + 1, h).start())
                    share(n_z - t - 1 if way == 0 else t + 1, h).start()

                when(takes(way, t, h, z), arrived)

    def regional_block(d, first=False):
        zz = lax.rem(z + d, n_z)
        for h in range(NH):
            shared_arrived(d, h)
        part = jnp.dot(
            reginv[:, pl.ds(pl.multiple_of(zz * 2 * kc, 2 * kc), 2 * kc)], xbuf[zz],
            preferred_element_type=F32,
        )
        regional[...] = part if first else regional[...] + part

    reg_load.wait()
    regional_block(0, True)
    step(0)

    pltpu.make_async_copy(rs_recv, rs_recv, rs_rs).wait()
    total = rs_chip[z]
    for k in range(n_z - 1):
        total += rs_recv[k].astype(F32)
    gath[xx, 0] = total.astype(BF16)

    by_distance = sorted(range(n_y), key=lambda d: (min(d, n_y - d), d))
    place_of = {d: n for n, d in enumerate(by_distance)}
    n_near_y = n_y // 2 + 1

    def near(k):
        return place_of[k] < n_near_y

    def y_copy(k):
        to = lax.rem(y + k, n_y)
        return pltpu.make_async_remote_copy(
            gath.at[xx, 0], gath.at[xx, place_of[n_y - k]], py_ss, py_rs.at[0 if near(k) else 1],
            device_id=(s, to * NX + xx), device_id_type=MESH,
        )

    groups = (pl.ds(0, n_near_y), pl.ds(n_near_y, n_y - n_near_y))

    def x_copy(k, part):
        to = lax.rem(xx + k, NX)
        ref = gath.at[xx, groups[part]]
        return pltpu.make_async_remote_copy(
            ref, ref, px_ss, px_rs, device_id=(s, y * NX + to), device_id_type=MESH
        )

    for k in by_distance[1:]:
        y_copy(k).start()

    regional_block(1)
    regional_block(n_z - 1)
    step(1, range(NH // 2))

    others_y = gath.at[0, pl.ds(0, n_y - 1)]
    for part, first in enumerate((1, n_near_y)):
        arrived_y = gath.at[0, pl.ds(first, (n_near_y if part == 0 else n_y) - first)]
        pltpu.make_async_copy(arrived_y, arrived_y, py_rs.at[part]).wait()
        for k in range(1, NX):
            x_copy(k, part).start()

    step(1, range(NH // 2, NH))
    regional_block(2)
    regional_block(n_z - 2)

    root_load.wait()
    others_x = gath.at[pl.ds(0, NX - 1)]
    pltpu.make_async_copy(others_x, others_x, px_rs).wait()
    zero = jnp.zeros((half, 128), BF16)
    lowb = lax.broadcasted_iota(jnp.int32, (half, 128), 1) < 64
    both = []
    for v in range(n_y):
        for u in range(NX):
            packed = gath[u, y_rank(lax.rem(v - y + n_y, n_y))]
            both += [jnp.where(lowb, packed, zero), jnp.where(lowb, zero, packed)]
    sol = jnp.dot(rootinv[...], jnp.concatenate(both, axis=0), preferred_element_type=F32)
    sol = sol + pltpu.roll(sol, 64, 1)
    sols[c, z] = jnp.where(low, sol[:half], sol[half:]).astype(BF16)

    def sol_copy(k):
        to = lax.rem(z + k, n_z)
        return pltpu.make_async_remote_copy(
            sols.at[c, z], sols.at[c, z], so_ss, so_rs, device_id=(2 * to + c, g), device_id_type=MESH
        )

    @pl.loop(1, n_z)
    def _(k):
        sol_copy(k).start()

    step(2)

    for j in range(4):
        @pl.when(has[j])
        def _():
            ref = margins.at[pl.ds(j * margin, margin)]
            pltpu.make_async_copy(ref, ref, lent_recv.at[j]).wait()

    local[...] += jnp.dot(inv[:, owned:], margins[...], preferred_element_type=F32)
    for d in (3, n_z - 3):
        regional_block(d)

    step(3)

    others_sol = sols.at[0, pl.ds(0, n_z - 1)]
    pltpu.make_async_copy(others_sol, others_sol, so_rs).wait()
    sol_pair = pltpu.make_async_remote_copy(
        sols.at[c], sols.at[c], pair_sem.at[2], pair_sem.at[3], device_id=(sib, g), device_id_type=MESH
    )
    sol_pair.start()
    regional_block(n_z // 2)
    other_core = sols.at[1 - c]
    pltpu.make_async_copy(other_core, other_core, pair_sem.at[3]).wait()
    for zz in range(n_z):
        p0 = sols[0, zz].astype(F32)
        p1 = sols[1, zz].astype(F32)
        top = jnp.where(low, p0, pltpu.roll(p1, 64, 1))
        bot = jnp.where(low, pltpu.roll(p0, 64, 1), p1)
        rsol = jnp.concatenate([top, bot], axis=0).astype(BF16)
        cols = slice(zz * 128, (zz + 1) * 128)
        regional[:, cols] += contract_rows(rmap[...], rsol)

    n_out = 4
    stores = []
    for n in range(n_out):
        width = n_cols // n_out
        cols = slice(n * width, (n + 1) * width)
        w = regional[:, cols].astype(BF16)
        out[:, cols] = (
            local[:, cols] + jnp.dot(basis[...], w, preferred_element_type=F32)
        ).astype(BF16)
        store = pltpu.make_async_copy(
            out.at[:, pl.ds(n * width, width)], out_hbm.at[:, pl.ds(n * width, width)], out_sem.at[n]
        )
        store.start()
        stores.append(store)

    for h in range(NH):
        for way in range(2):
            for t in range(last + 1):
                if t > 0 or h == NH - 1:
                    when(takes(way, t, h, chip_to[way]), lambda: ring(way, t, h).wait_send())
        for d in range(n_z):
            share(d, h).wait_send()
    for j in range(4):
        @pl.when(has[j])
        def _():
            lent_copy(j).wait_send()
    pltpu.make_async_copy(rs_recv, rs_recv, rs_ss).wait()
    pair.wait_send()
    sol_pair.wait_send()
    pltpu.make_async_copy(others_y, others_y, py_ss).wait()
    pltpu.make_async_copy(others_x, others_x, px_ss).wait()
    pltpu.make_async_copy(others_sol, others_sol, so_ss).wait()
    for store in stores:
        store.wait()


def per_device(n_sub, n_region, residual, send_rows, local_inverse, coarse_basis, regional_inverse, root_map, root_inverse):
    args = (
        residual[0, 0], send_rows[0, 0], local_inverse[0, 0], coarse_basis[0, 0],
        regional_inverse[0, 0], root_map[0, 0].T, root_inverse[0],
    )
    res, rows, inv, basis, reginv, rmap, rootinv = args
    owned, cols = res.shape
    kr, kc = rmap.shape
    margin = rows.shape[1]
    n_z = n_sub // 2
    dma = pltpu.SemaphoreType.DMA
    flops = 2 * cols * (owned * inv.shape[1] + kc * reginv.shape[1] + 2 * kc * owned + 4 * kr * kc + 4 * margin * owned)
    out = pl.pallas_call(
        functools.partial(kernel, n_sub, n_region),
        out_shape=jax.ShapeDtypeStruct((owned, cols), BF16),
        in_specs=[pl.BlockSpec(memory_space=pl.ANY)] * 7,
        out_specs=pl.BlockSpec(memory_space=pl.ANY),
        scratch_shapes=[pltpu.VMEM(a.shape, a.dtype) for a in args]
        + [
            pltpu.VMEM((n_z, 2 * kc, cols), BF16),
            pltpu.VMEM((4 * margin, cols), BF16),
            pltpu.VMEM((4 * margin, cols), BF16),
            pltpu.VMEM((2, n_z, kr // 2, 128), F32),
            pltpu.VMEM((n_z, kr // 2, 128), F32),
            pltpu.VMEM((n_z, kr // 2, 128), F32),
            pltpu.VMEM((n_z, kr // 2, 128), BF16),
            pltpu.VMEM((n_z - 1, kr // 2, 128), BF16),
            pltpu.VMEM((NX, n_region // NX, kr // 2, 128), BF16),
            pltpu.VMEM((2, n_z, kr // 2, 128), BF16),
            pltpu.VMEM((kc, cols), F32),
            pltpu.VMEM((owned, cols), F32),
            pltpu.VMEM((owned, cols), BF16),
            dma((6 + NH,)), dma((4,)),
            dma((2, n_z // 2, NH)), dma((2, n_z // 2, NH)),
            dma((n_z, NH)), dma((n_z, NH)),
            dma((4,)), dma((4,)),
            *[dma] * 3, dma((2,)), *[dma] * 4,
            dma((4,)),
            *[pltpu.SemaphoreType.REGULAR] * 3,
        ],
        compiler_params=pltpu.CompilerParams(
            collective_id=0, has_side_effects=True, vmem_limit_bytes=60 * 1024 * 1024
        ),
        cost_estimate=pl.CostEstimate(flops=flops, bytes_accessed=4 << 20, transcendentals=0),
    )(*args)
    return out.reshape(1, 1, owned, cols)


def solution(mesh):
    here = P("sub", "region", None, None)
    return jax.shard_map(
        functools.partial(per_device, mesh.shape["sub"], mesh.shape["region"]),
        mesh=mesh,
        in_specs=(here,) * 6 + (P("region", None, None),),
        out_specs=here,
        check_vma=False,
    )
```

```python
import functools

import jax
import jax.numpy as jnp
from jax import lax
from jax.experimental import pallas as pl
from jax.experimental.pallas import tpu as pltpu
from jax.sharding import PartitionSpec as P

F32 = jnp.float32
BF16 = jnp.bfloat16
MESH = pl.DeviceIdType.MESH
NH = 2
NX = 4


def contract_rows(a, b):
    return lax.dot_general(a, b, (((0,), (0,)), ((), ())), preferred_element_type=F32)


def kernel(
    n_sub, n_region,
    res_hbm, rows_hbm, inv_hbm, basis_hbm, reg_hbm, map_hbm, root_hbm, out_hbm,
    res, rows, inv, basis, reginv, rmap, rootinv,
    xbuf, lent, margins, rs_part, rs_pair, rs_chip, rs_send, rs_recv, gath, sols, regional, local, out,
    in_sem, out_sem, ring_send, ring_recv, share_send, share_recv,
    lent_send, lent_recv, rs_ss, rs_rs, py_ss, py_rs, px_ss, px_rs, so_ss, so_rs,
    pair_sem, ready_near, ready_col, ready_plane,
):
    s = lax.axis_index("sub")
    g = lax.axis_index("region")
    n_z = n_sub // 2
    n_y = n_region // NX
    z, c = s // 2, s % 2
    y, xx = g // NX, g % NX
    sib = s + 1 - 2 * c
    n_cols = res.shape[1]
    kc = basis.shape[1]
    wide = n_cols // NH
    margin = rows.shape[1]
    owned = res.shape[0]

    def piece(ref, h):
        return ref.at[:, pl.ds(h * wide, wide)]

    basis_load = pltpu.make_async_copy(basis_hbm, basis, in_sem.at[0])
    res_loads = [pltpu.make_async_copy(piece(res_hbm, h), piece(res, h), in_sem.at[1 + h]) for h in range(NH)]
    map_load, rows_load, inv_load, reg_load, root_load = [
        pltpu.make_async_copy(a, b, in_sem.at[1 + NH + i])
        for i, (a, b) in enumerate(
            ((map_hbm, rmap), (rows_hbm, rows), (inv_hbm, inv), (reg_hbm, reginv), (root_hbm, rootinv))
        )
    ]
    for load in (basis_load, *res_loads, map_load, rows_load, inv_load, reg_load, root_load):
        load.start()

    barrier = pltpu.get_barrier_semaphore()

    def signal(sem, to):
        pl.semaphore_signal(sem, inc=1, device_id=to, device_id_type=MESH)

    def wait_for(sem, n):
        pl.when(n > 0)(lambda: pl.semaphore_wait(sem, n))

    def y_rank(v):
        far = jnp.minimum(v, n_y - v)
        return jnp.where(v == 0, 0, 2 * far - 1 + jnp.where(v > n_y // 2, 1, 0))

    my_rank = y_rank(y)
    before_far = jnp.logical_and(xx == 0, y > 0)
    after_far = jnp.logical_and(xx == NX - 1, y < n_y - 1)
    plane = [((s, v * NX + xx), y != v, y_rank(v) > my_rank) for v in range(n_y)]
    plane += [((s, y * NX + v), xx != v, xx < v) for v in range(NX)]
    plane += [
        ((s, g - 1), before_far, y_rank(y - 1) > my_rank),
        ((s, g + 1), after_far, y_rank(y + 1) > my_rank),
    ]
    higher = [jnp.logical_and(there, up) for _, there, up in plane]
    lower = [jnp.logical_and(there, jnp.logical_not(up)) for _, there, up in plane]

    def count(flags):
        return sum(jnp.where(f, 1, 0) for f in flags)

    @pl.loop(z + 1, n_z)
    def _(to):
        signal(barrier, (2 * to + c, g))

    pl.when(c == 0)(lambda: signal(barrier, (sib, g)))
    across_down = jnp.logical_and(c == 0, z > 0)
    across_up = jnp.logical_and(c == 1, z < n_z - 1)
    pl.when(across_up)(lambda: signal(barrier, (s + 1, g)))

    for (to, _, _), up in zip(plane, higher):
        @pl.when(up)
        def _():
            signal(barrier, to)

    wait_for(barrier, z + c + count([across_down, *lower]))

    pl.when(z > 0)(lambda: signal(ready_near, (s - 2, g)))
    pl.when(c == 1)(lambda: signal(ready_near, (sib, g)))

    @pl.loop(0, z - 1)
    def _(to):
        signal(ready_col, (2 * to + c, g))

    pl.when(across_down)(lambda: signal(ready_col, (s - 1, g)))

    for (to, _, _), low_one in zip(plane, lower):
        @pl.when(low_one)
        def _():
            signal(ready_plane, to)

    n_near = count([z < n_z - 1, c == 0])
    n_far = jnp.maximum(n_z - 2 - z, 0) + count([across_up])

    core_rows = pl.ds(pl.multiple_of(c * kc, kc), kc)

    def block(zz, h):
        return xbuf.at[zz, core_rows, pl.ds(h * wide, wide)]

    def ring(way, t, h):
        to = lax.rem(z + (1 if way == 0 else n_z - 1), n_z)
        zz = lax.rem(z + (n_z - t if way == 0 else t), n_z)
        ref = block(zz, h)
        return pltpu.make_async_remote_copy(
            ref, ref, ring_send.at[way, t, h], ring_recv.at[way, t, h],
            device_id=(2 * to + c, g), device_id_type=MESH,
        )

    def ring_arrived(way, t, h):
        zz = lax.rem(z + (n_z - t - 1 if way == 0 else t + 1), n_z)
        ref = block(zz, h)
        pltpu.make_async_copy(ref, ref, ring_recv.at[way, t, h]).wait()

    def share(d, h):
        ref = block(lax.rem(z + d, n_z), h)
        return pltpu.make_async_remote_copy(
            ref, ref, share_send.at[d, h], share_recv.at[d, h],
            device_id=(sib, g), device_id_type=MESH,
        )

    def shared_arrived(d, h):
        zz = lax.rem(z + d, n_z)
        ref = xbuf.at[zz, pl.ds(pl.multiple_of((1 - c) * kc, kc), kc), pl.ds(h * wide, wide)]
        pltpu.make_async_copy(ref, ref, share_recv.at[d, h]).wait()

    last = n_z // 2 - 1

    def takes(way, t, h, to):
        if t < last:
            return None
        if (h < NH // 2) == (way == 0):
            return None if way == 1 else to != 0
        return to == 0 if way == 1 else False

    def when(cond, then):
        if cond is None:
            then()
        elif cond is not False:
            pl.when(cond)(then)

    chip_to = (lax.rem(z + 1, n_z), lax.rem(z + n_z - 1, n_z))

    basis_load.wait()
    for h in range(NH):
        res_loads[h].wait()
        cols = slice(h * wide, (h + 1) * wide)
        xbuf[z, core_rows, cols] = contract_rows(basis[...], res[:, cols]).astype(BF16)
        if h == 0:
            wait_for(ready_near, n_near)
            ring(0, 0, 0).start()
            pl.when(z > 0)(lambda: ring(1, 0, 0).start())
        share(0, h).start()

    map_load.wait()
    proj = jnp.dot(rmap[...], xbuf[z, core_rows, :], preferred_element_type=F32)
    half = proj.shape[0] // 2
    low = lax.broadcasted_iota(jnp.int32, (half, 128), 1) < 64
    for zz in range(n_z):
        top = proj[:half, zz * 128:(zz + 1) * 128]
        bot = proj[half:, zz * 128:(zz + 1) * 128]
        rs_part[0, zz] = jnp.where(low, top, pltpu.roll(bot, 64, 1))
        rs_part[1, zz] = jnp.where(low, pltpu.roll(top, 64, 1), bot)

    pair = pltpu.make_async_remote_copy(
        rs_part.at[1 - c], rs_pair, pair_sem.at[0], pair_sem.at[1], device_id=(sib, g), device_id_type=MESH
    )
    pair.start()
    pair.wait_recv()
    rs_chip[...] = rs_part[c] + rs_pair[...]
    rs_send[...] = rs_chip[...].astype(BF16)

    def rs_copy(to):
        return pltpu.make_async_remote_copy(
            rs_send.at[to], rs_recv.at[lax.rem(to - z + n_z, n_z) - 1], rs_ss, rs_rs,
            device_id=(2 * to + c, g), device_id_type=MESH,
        )

    @pl.loop(0, z)
    def _(to):
        rs_copy(to).start()

    def follow(way):
        for h in range(1, NH):
            ring(way, 0, h - 1).wait_send()
            ring(way, 0, h).start()

    follow(0)
    pl.when(z > 0)(lambda: follow(1))
    wait_for(ready_col, n_far)

    @pl.when(z == 0)
    def _():
        ring(1, 0, 0).start()

    @pl.loop(z + 1, n_z)
    def _(to):
        rs_copy(to).start()

    rows_load.wait()

    def lent_copy(j):
        to = ((s - 1, g), (s + 1, g), (s, g - 1), (s, g + 1))[j]
        place = (1, 0, 3, 2)[j]
        return pltpu.make_async_remote_copy(
            lent.at[pl.ds(j * margin, margin)], margins.at[pl.ds(place * margin, margin)],
            lent_send.at[j], lent_recv.at[place], device_id=to, device_id_type=MESH,
        )

    has = (s > 0, s < n_sub - 1, g > 0, g < n_region - 1)
    for j in range(4):
        if j == 2:
            wait_for(ready_plane, count(higher))
        row_id = lax.broadcasted_iota(jnp.int32, (owned, margin), 0)
        pick = jnp.where(row_id == rows[pl.ds(j, 1), :], 1.0, 0.0).astype(BF16)
        lent[pl.ds(j * margin, margin), :] = contract_rows(pick, res[...]).astype(BF16)

        @pl.when(has[j])
        def _():
            lent_copy(j).start()

        @pl.when(jnp.logical_not(has[j]))
        def _():
            margins[pl.ds(j * margin, margin), :] = jnp.zeros((margin, n_cols), BF16)

    pl.when(z == 0)(lambda: follow(1))

    inv_load.wait()
    local[...] = jnp.dot(inv[:, :owned], res[...], preferred_element_type=F32)

    def step(t, pieces=range(NH)):
        for h in pieces:
            for way in (1, 0):
                def arrived():
                    ring_arrived(way, t, h)
                    if t < last:
                        when(takes(way, t + 1, h, chip_to[way]), lambda: ring(way, t + 1, h).start())
                    share(n_z - t - 1 if way == 0 else t + 1, h).start()

                when(takes(way, t, h, z), arrived)

    def regional_block(d, first=False):
        zz = lax.rem(z + d, n_z)
        for h in range(NH):
            shared_arrived(d, h)
        part = jnp.dot(
            reginv[:, pl.ds(pl.multiple_of(zz * 2 * kc, 2 * kc), 2 * kc)], xbuf[zz],
            preferred_element_type=F32,
        )
        regional[...] = part if first else regional[...] + part

    reg_load.wait()
    regional_block(0, True)
    step(0)

    pltpu.make_async_copy(rs_recv, rs_recv, rs_rs).wait()
    total = rs_chip[z]
    for k in range(n_z - 1):
        total += rs_recv[k].astype(F32)
    gath[xx, 0] = total.astype(BF16)

    by_distance = sorted(range(n_y), key=lambda d: (min(d, n_y - d), d))
    place_of = {d: n for n, d in enumerate(by_distance)}
    n_near_y = n_y // 2 + 1

    def near(k):
        return place_of[k] < n_near_y

    def y_copy(k):
        to = lax.rem(y + k, n_y)
        return pltpu.make_async_remote_copy(
            gath.at[xx, 0], gath.at[xx, place_of[n_y - k]], py_ss, py_rs.at[0 if near(k) else 1],
            device_id=(s, to * NX + xx), device_id_type=MESH,
        )

    groups = (pl.ds(0, n_near_y), pl.ds(n_near_y, n_y - n_near_y))

    def x_copy(k, part):
        to = lax.rem(xx + k, NX)
        ref = gath.at[xx, groups[part]]
        return pltpu.make_async_remote_copy(
            ref, ref, px_ss, px_rs, device_id=(s, y * NX + to), device_id_type=MESH
        )

    for k in by_distance[1:]:
        y_copy(k).start()

    regional_block(1)
    regional_block(n_z - 1)
    step(1, range(NH // 2))

    others_y = gath.at[0, pl.ds(0, n_y - 1)]
    for part, first in enumerate((1, n_near_y)):
        arrived_y = gath.at[0, pl.ds(first, (n_near_y if part == 0 else n_y) - first)]
        pltpu.make_async_copy(arrived_y, arrived_y, py_rs.at[part]).wait()
        for k in range(1, NX):
            x_copy(k, part).start()

    step(1, range(NH // 2, NH))
    regional_block(2)
    regional_block(n_z - 2)

    root_load.wait()
    others_x = gath.at[pl.ds(0, NX - 1)]
    pltpu.make_async_copy(others_x, others_x, px_rs).wait()
    zero = jnp.zeros((half, 128), BF16)
    lowb = lax.broadcasted_iota(jnp.int32, (half, 128), 1) < 64
    both = []
    for v in range(n_y):
        for u in range(NX):
            packed = gath[u, y_rank(lax.rem(v - y + n_y, n_y))]
            both += [jnp.where(lowb, packed, zero), jnp.where(lowb, zero, packed)]
    sol = jnp.dot(rootinv[...], jnp.concatenate(both, axis=0), preferred_element_type=F32)
    sol = sol + pltpu.roll(sol, 64, 1)
    sols[c, z] = jnp.where(low, sol[:half], sol[half:]).astype(BF16)

    def sol_copy(k):
        to = lax.rem(z + k, n_z)
        return pltpu.make_async_remote_copy(
            sols.at[c, z], sols.at[c, z], so_ss, so_rs, device_id=(2 * to + c, g), device_id_type=MESH
        )

    @pl.loop(1, n_z)
    def _(k):
        sol_copy(k).start()

    step(2)

    for j in range(4):
        @pl.when(has[j])
        def _():
            ref = margins.at[pl.ds(j * margin, margin)]
            pltpu.make_async_copy(ref, ref, lent_recv.at[j]).wait()

    local[...] += jnp.dot(inv[:, owned:], margins[...], preferred_element_type=F32)
    for d in (3, n_z - 3):
        regional_block(d)

    step(3)

    others_sol = sols.at[0, pl.ds(0, n_z - 1)]
    pltpu.make_async_copy(others_sol, others_sol, so_rs).wait()
    sol_pair = pltpu.make_async_remote_copy(
        sols.at[c], sols.at[c], pair_sem.at[2], pair_sem.at[3], device_id=(sib, g), device_id_type=MESH
    )
    sol_pair.start()
    regional_block(n_z // 2)
    other_core = sols.at[1 - c]
    pltpu.make_async_copy(other_core, other_core, pair_sem.at[3]).wait()
    for zz in range(n_z):
        p0 = sols[0, zz].astype(F32)
        p1 = sols[1, zz].astype(F32)
        top = jnp.where(low, p0, pltpu.roll(p1, 64, 1))
        bot = jnp.where(low, pltpu.roll(p0, 64, 1), p1)
        rsol = jnp.concatenate([top, bot], axis=0).astype(BF16)
        cols = slice(zz * 128, (zz + 1) * 128)
        regional[:, cols] += contract_rows(rmap[...], rsol)

    n_out = 4
    stores = []
    for n in range(n_out):
        width = n_cols // n_out
        cols = slice(n * width, (n + 1) * width)
        w = regional[:, cols].astype(BF16)
        out[:, cols] = (
            local[:, cols] + jnp.dot(basis[...], w, preferred_element_type=F32)
        ).astype(BF16)
        store = pltpu.make_async_copy(
            out.at[:, pl.ds(n * width, width)], out_hbm.at[:, pl.ds(n * width, width)], out_sem.at[n]
        )
        store.start()
        stores.append(store)

    for h in range(NH):
        for way in range(2):
            for t in range(last + 1):
                if t > 0 or h == NH - 1:
                    when(takes(way, t, h, chip_to[way]), lambda: ring(way, t, h).wait_send())
        for d in range(n_z):
            share(d, h).wait_send()
    for j in range(4):
        @pl.when(has[j])
        def _():
            lent_copy(j).wait_send()
    pltpu.make_async_copy(rs_recv, rs_recv, rs_ss).wait()
    pair.wait_send()
    sol_pair.wait_send()
    pltpu.make_async_copy(others_y, others_y, py_ss).wait()
    pltpu.make_async_copy(others_x, others_x, px_ss).wait()
    pltpu.make_async_copy(others_sol, others_sol, so_ss).wait()
    for store in stores:
        store.wait()


def per_device(n_sub, n_region, residual, send_rows, local_inverse, coarse_basis, regional_inverse, root_map, root_inverse):
    args = (
        residual[0, 0], send_rows[0, 0], local_inverse[0, 0], coarse_basis[0, 0],
        regional_inverse[0, 0], root_map[0, 0].T, root_inverse[0],
    )
    res, rows, inv, basis, reginv, rmap, rootinv = args
    owned, cols = res.shape
    kr, kc = rmap.shape
    margin = rows.shape[1]
    n_z = n_sub // 2
    dma = pltpu.SemaphoreType.DMA
    flops = 2 * cols * (owned * inv.shape[1] + kc * reginv.shape[1] + 2 * kc * owned + 4 * kr * kc + 4 * margin * owned)
    out = pl.pallas_call(
        functools.partial(kernel, n_sub, n_region),
        out_shape=jax.ShapeDtypeStruct((owned, cols), BF16),
        in_specs=[pl.BlockSpec(memory_space=pl.ANY)] * 7,
        out_specs=pl.BlockSpec(memory_space=pl.ANY),
        scratch_shapes=[pltpu.VMEM(a.shape, a.dtype) for a in args]
        + [
            pltpu.VMEM((n_z, 2 * kc, cols), BF16),
            pltpu.VMEM((4 * margin, cols), BF16),
            pltpu.VMEM((4 * margin, cols), BF16),
            pltpu.VMEM((2, n_z, kr // 2, 128), F32),
            pltpu.VMEM((n_z, kr // 2, 128), F32),
            pltpu.VMEM((n_z, kr // 2, 128), F32),
            pltpu.VMEM((n_z, kr // 2, 128), BF16),
            pltpu.VMEM((n_z - 1, kr // 2, 128), BF16),
            pltpu.VMEM((NX, n_region // NX, kr // 2, 128), BF16),
            pltpu.VMEM((2, n_z, kr // 2, 128), BF16),
            pltpu.VMEM((kc, cols), F32),
            pltpu.VMEM((owned, cols), F32),
            pltpu.VMEM((owned, cols), BF16),
            dma((6 + NH,)), dma((4,)),
            dma((2, n_z // 2, NH)), dma((2, n_z // 2, NH)),
            dma((n_z, NH)), dma((n_z, NH)),
            dma((4,)), dma((4,)),
            *[dma] * 3, dma((2,)), *[dma] * 4,
            dma((4,)),
            *[pltpu.SemaphoreType.REGULAR] * 3,
        ],
        compiler_params=pltpu.CompilerParams(
            collective_id=0, has_side_effects=True, vmem_limit_bytes=60 * 1024 * 1024
        ),
        cost_estimate=pl.CostEstimate(flops=flops, bytes_accessed=4 << 20, transcendentals=0),
    )(*args)
    return out.reshape(1, 1, owned, cols)


def solution(mesh):
    here = P("sub", "region", None, None)
    return jax.shard_map(
        functools.partial(per_device, mesh.shape["sub"], mesh.shape["region"]),
        mesh=mesh,
        in_specs=(here,) * 6 + (P("region", None, None),),
        out_specs=here,
        check_vma=False,
    )
```
